256 devices in a mesh: grp: 2 (over core), exp: 16 (over x, y), hid: 8 (over z).
Axes of the slice: x: 4, y: 4, z: 8, core: 2. Of those that a mesh axis runs over, the one named last changes fastest.
Arguments:
- queries: bfloat16 [1024, 48, 128], P(('grp', 'exp', 'hid')), may hold values from -150 to 150
- cache_keys: bfloat16 [1024, 256, 8, 128], P(('grp', 'exp', 'hid')), may hold values from -8 to 8
- cache_values: bfloat16 [1024, 256, 8, 128], P(('grp', 'exp', 'hid')), may hold values from -6 to 6
- new_keys: bfloat16 [1024, 8, 128], P(('grp', 'exp', 'hid')), may hold values from -8 to 8
- new_values: bfloat16 [1024, 8, 128], P(('grp', 'exp', 'hid')), may hold values from -6 to 6
- lengths: int32 [1024], P(('grp', 'exp', 'hid')), may hold values from 1 to 256, 131072 in all
- residual: bfloat16 [1024, 6144], P(('grp', 'exp', 'hid')), may hold values from -6 to 6
- norm_gain: float32 [6144], replicated, may hold values from 0.1 to 1.9
- routes: int32 [1024, 2], P(('grp', 'exp', 'hid')), may hold values from 0 to 7, all different within a row; in each aligned block of 4 rows (0 to 3, 4 to 7, ...) at most 2 rows name the same one
- gate_logits: float32 [1024, 2], P(('grp', 'exp', 'hid')), may hold values from -4 to 4
- w_gate: bfloat16 [8, 6144, 8192], P('hid', None, ('grp', 'exp')), may hold values from -0.078125 to 0.078125
- w_up: bfloat16 [8, 6144, 8192], P('hid', None, ('grp', 'exp')), may hold values from -0.078125 to 0.078125
- w_down: bfloat16 [8, 8192, 6144], P('hid', ('grp', 'exp')), may hold values from -0.0625 to 0.0625
Outputs:
- layer_out: bfloat16 [1024, 6144], P(('grp', 'exp', 'hid'))
The draws below stay inside these ranges and needn't reach their ends.
Inputs may be any that keep to these rules, and one draw needn't show every extreme that they name: `routes`: each row names two different experts; among the 4 rows of one device no expert is named more than 2 times, and some device names some expert exactly 2 times.
All inputs are finite; a program needn't handle non-finite values. No bound on the sum of `lengths` on one device may be relied on, other than what follows from the above.
Results may differ from the reference program's by a relative error of at most 0.015.
Values may be sent and summed in bfloat16 or wider, within the bound.
A program may use at most 128 MiB of HBM per device.

```python
import math
import jax
import jax.numpy as jnp
import numpy as np
from jax import lax

HEADS = 48
KV = 8
HD = 128
D = 6144
E = 8
TOP = 2
FF = 8192
REQ_DEV = 4
CTX = 256
CAP = 2
ROWS = 1024
N_GRP = 2
N_EXP = 16


def draw_new_keys(key, part):
    key = jax.random.fold_in(key, 1)
    values = jnp.clip(jax.random.normal(key, (ROWS, KV, HD), jnp.float32), -8.0, 8.0)
    return values.astype(jnp.bfloat16)


def draw_cache_keys(key, part):
    key = jax.random.fold_in(key, 2)
    values = jax.random.normal(key, (ROWS, CTX, KV, HD), jnp.float32)
    return jnp.clip(values, -8.0, 8.0).astype(jnp.bfloat16)


def draw_queries(key, part):
    key = jax.random.fold_in(key, 3)
    values = jnp.clip(jax.random.normal(key, (ROWS, HEADS, HD), jnp.float32), -8.0, 8.0)
    return values.astype(jnp.bfloat16)


def levels(own_key, extent, split, least, largest):
    gain = 1.0
    for dim, blocks in split:
        steps = jax.random.uniform(jax.random.fold_in(jax.random.fold_in(own_key, 6), dim), (blocks,), jnp.float32, least / len(split), largest / len(split))
        gain = gain * jnp.repeat(jnp.exp(steps), extent[dim] // blocks).reshape((-1,) + (1,) * (len(extent) - 1 - dim))
    return gain


def split_up(number_of, total, limit, slope):
    portions = [(1 << 20) // math.isqrt(grade ** slope) + 1 for grade in range(2, number_of + 1)]
    spare, counts = total - limit - (number_of - 1), [1] * (number_of - 1)
    while spare > 0:
        movable = [i for i in range(number_of - 1) if counts[i] < limit]
        whole, left = sum([portions[i] for i in movable]), spare
        for i in movable:
            addition = min(limit - counts[i], max(1, left * portions[i] // whole), spare)
            counts[i] = counts[i] + addition
            spare = spare - addition
    return np.array([limit] + counts)


def uneven_parts(stream_key, count, total, limit, lean):
    if count == 2:
        one = jax.random.randint(stream_key, (), max(1, total - limit), min(limit, total - 1) + 1)
        return jnp.stack([one, total - one])
    tallies = jnp.asarray(split_up(count, total, limit, lean), jnp.int32)
    twos = (count - 1) // 2
    source_of, receiver = tallies[1:1 + 2 * twos:2], tallies[2:2 + 2 * twos:2]
    room = jnp.minimum(source_of - 1, limit - receiver)
    passed = jax.random.randint(jax.random.fold_in(stream_key, 1), (twos,), 0, 1 << 20) % (room + 1)
    tallies = tallies.at[1:1 + 2 * twos:2].set(source_of - passed).at[2:2 + 2 * twos:2].set(receiver + passed)
    return tallies[jax.random.permutation(jax.random.fold_in(stream_key, 2), count)]


def assign_block(rng, own, number, rows, count, top, most, lean):
    order = jax.random.permutation(rng, count)
    heavy_load, ordinary = shares(count, rows * top, most, lean, True), shares(count, rows * top, most, lean, False)
    places = jnp.arange(count)

    def named(tallies, offset_by):
        used = int((tallies > 0).sum())
        fixed = max(1, used // 4)
        passed = fixed + (places - fixed + offset_by * (used - fixed)) % max(1, count - fixed)
        return jnp.zeros((count,), jnp.int32).at[order[jnp.where(places < fixed, places, passed)]].set(jnp.asarray(tallies, jnp.int32))

    tallies = jnp.where(number % 4 == 0, named(heavy_load, number // 4), named(ordinary, number - number // 4 - 1))
    mixed = jax.random.permutation(jax.random.fold_in(own, 3), count)
    giver, sink = mixed[0:count // 2 * 2:2], mixed[1:count // 2 * 2:2]
    slack = jnp.minimum(tallies[giver] - 1, most - tallies[sink]) // 2
    slack = jnp.where((giver == order[0]) | (sink == order[0]) | (tallies[sink] == 0), 0, jnp.maximum(slack, 0))
    passed = jax.random.randint(jax.random.fold_in(own, 4), (count // 2,), 0, 1 << 20) % (slack + 1)
    tallies = tallies.at[giver].add(-passed).at[sink].add(passed)
    members = jnp.searchsorted(jnp.cumsum(tallies), jnp.arange(rows * top), side="right").astype(jnp.int32)
    grid = members.reshape(top, rows).T
    grid = grid[jax.random.permutation(jax.random.fold_in(own, 1), rows)]
    offset_by = jax.random.randint(jax.random.fold_in(own, 2), (rows, 1), 0, top)
    return jnp.take_along_axis(grid, (jnp.arange(top)[None, :] + offset_by) % top, axis=1)


def shares(count, total, most, skew, full):
    loads = [(1 << 20) // math.isqrt(grade ** skew) + 1 for grade in range(1, count + 1)]
    largest = most if full else min(most, max(-(-total // count), total * loads[0] // sum(loads)))
    least = 1 if total - largest >= count - 1 else 0
    given, spare = [largest] + [least] * (count - 1), total - largest - least * (count - 1)
    while spare > 0:
        free = [i for i in range(1, count) if given[i] < largest] or [i for i in range(1, count) if given[i] < most]
        pool, budget = sum([loads[i] for i in free]), spare
        for i in free:
            addition = min(most - given[i], max(1, budget * loads[i] // pool), spare)
            given[i] = given[i] + addition
            spare = spare - addition
    return np.array(given)


def bell_draw(own_key, shape, deviation, most, pieces=(), held_as=jnp.bfloat16):
    values = jax.random.normal(own_key, shape, jnp.float32) * deviation
    if len(pieces) > 0:
        values = levels(own_key, shape, pieces, -0.22, 0.18) * values
    return jnp.clip(values, min=-most, max=most).astype(held_as)


def setup_inputs(seed: int = 0) -> dict:
    arg_keys = jax.random.split(jax.random.key(seed), 14)
    queries = draw_queries(jax.random.fold_in(arg_keys[13], 71), 0)
    cache_keys = draw_cache_keys(jax.random.fold_in(arg_keys[13], 71), 0)
    cache_values = bell_draw(arg_keys[2], (ROWS, CTX, KV, HD), 1.0, 6.0, ((0, 256),))
    new_keys = draw_new_keys(jax.random.fold_in(arg_keys[13], 71), 0)
    new_values = bell_draw(arg_keys[4], (ROWS, KV, HD), 1.0, 6.0, ((0, 256),))
    lengths = uneven_parts(arg_keys[5], ROWS, ROWS * CTX // 2, CTX, 2).astype(jnp.int32)
    residual = bell_draw(arg_keys[6], (ROWS, D), 1.0, 6.0, ((0, 256),))
    norm_gain = jnp.clip(1.0 + 0.18 * jax.random.normal(arg_keys[7], (D,), jnp.float32), 0.1, 1.9)
    routes_keys = jax.random.split(jax.random.fold_in(arg_keys[8], 1), ROWS // REQ_DEV)
    routes_turns = jax.random.permutation(jax.random.fold_in(arg_keys[8], 3), ROWS // REQ_DEV)
    routes = jax.vmap(lambda own, number: assign_block(jax.random.fold_in(arg_keys[8], 2), own, number, REQ_DEV, E, TOP, CAP, 2))(routes_keys, routes_turns).reshape((ROWS, TOP))
    gate_logits = bell_draw(arg_keys[9], (ROWS, TOP), 1.0, 4.0, ((0, 256),), jnp.float32)
    w_gate = bell_draw(arg_keys[10], (E, D, FF), D ** -0.5, 0.078125, ((0, 8), (2, 32)))
    w_up = bell_draw(arg_keys[11], (E, D, FF), D ** -0.5, 0.078125, ((0, 8), (2, 32)))
    w_down = bell_draw(arg_keys[12], (E, FF, D), FF ** -0.5, 0.0625, ((0, 8), (1, 32)))
    return dict(queries=queries, cache_keys=cache_keys, cache_values=cache_values, new_keys=new_keys, new_values=new_values, lengths=lengths, residual=residual, norm_gain=norm_gain, routes=routes, gate_logits=gate_logits, w_gate=w_gate, w_up=w_up, w_down=w_down)


def attend(queries, cache_keys, cache_values, new_keys, new_values, lengths):
    count = queries.shape[0]
    group = HEADS // KV
    qvals = queries.reshape(count, KV, group, HD).astype(jnp.float32)
    score_scale = 1.0 / math.sqrt(HD)
    cached = jnp.einsum('rkgd,rtkd->rkgt', qvals, cache_keys.astype(jnp.float32)) * score_scale
    fresh = jnp.einsum('rkgd,rkd->rkg', qvals, new_keys.astype(jnp.float32)) * score_scale
    positions = jnp.arange(CTX, dtype=jnp.int32)
    valid = positions[None, :] < lengths[:, None]
    cached = jnp.where(valid[:, None, None, :], cached, jnp.float32(-1e+30))
    highest = jnp.maximum(lax.optimization_barrier(jnp.max(cached, axis=-1)), fresh)
    cached_exp = jnp.exp(cached - highest[..., None])
    fresh_exp = jnp.exp(fresh - highest)
    total = lax.optimization_barrier(jnp.sum(cached_exp, axis=-1)) + fresh_exp
    cached_w = (cached_exp / total[..., None]).astype(jnp.bfloat16)
    fresh_w = (fresh_exp / total).astype(jnp.bfloat16)
    result = jnp.einsum('rkgt,rtkd->rkgd', cached_w.astype(jnp.float32), cache_values.astype(jnp.float32))
    result = result + fresh_w.astype(jnp.float32)[..., None] * new_values.astype(jnp.float32)[:, :, None, :]
    return result.reshape(count, D).astype(jnp.bfloat16)

def reference(queries, cache_keys, cache_values, new_keys, new_values, lengths, residual, norm_gain, routes, gate_logits, w_gate, w_up, w_down):
    attended = attend(queries, cache_keys, cache_values, new_keys, new_values, lengths)
    mixed = residual.astype(jnp.float32) + attended.astype(jnp.float32)
    normed = (mixed * lax.rsqrt(lax.optimization_barrier(jnp.mean(mixed * mixed, axis=-1, keepdims=True)) + 1e-05) * norm_gain).astype(jnp.bfloat16)
    gates = jax.nn.softmax(gate_logits, axis=-1)
    slices = N_GRP * N_EXP
    slice_size = FF // slices

    def one_expert(index):
        gate_in = jnp.dot(normed, w_gate[index], preferred_element_type=jnp.float32)
        up_in = jnp.dot(normed, w_up[index], preferred_element_type=jnp.float32)
        hidden = (jax.nn.silu(gate_in) * up_in).astype(jnp.bfloat16)
        hidden_parts = hidden.reshape(ROWS, slices, slice_size).astype(jnp.float32)
        down_parts = w_down[index].reshape(slices, slice_size, D).astype(jnp.float32)
        partial_value = jnp.einsum('rsh,shd->rsd', hidden_parts, down_parts).astype(jnp.bfloat16)
        return lax.optimization_barrier(jnp.sum(partial_value.astype(jnp.float32), axis=1)).astype(jnp.bfloat16)
    expert_out = lax.map(one_expert, jnp.arange(E, dtype=jnp.int32))
    expert_ids = jnp.arange(E, dtype=jnp.int32)
    chosen = routes[:, :, None] == expert_ids[None, None, :]
    combine = lax.optimization_barrier(jnp.sum(jnp.where(chosen, gates[:, :, None], jnp.float32(0.0)), axis=1))
    moe = jnp.einsum('re,erd->rd', combine, expert_out.astype(jnp.float32))
    return (mixed + moe).astype(jnp.bfloat16)
```

```python
import functools
import math

import jax
import jax.numpy as jnp
from jax import lax
from jax.experimental import pallas as pl
from jax.experimental.pallas import tpu as pltpu
from jax.sharding import PartitionSpec as P

CAP = 2
SIDE = 4
MESH = pl.DeviceIdType.MESH


def attend(queries, cache_keys, cache_values, new_keys, new_values, lengths):
    count = queries.shape[0]
    kv_heads = cache_keys.shape[2]
    head_size = cache_keys.shape[3]
    slots_cached = cache_keys.shape[1]
    group = queries.shape[1] // kv_heads
    qvals = queries.reshape(count, kv_heads, group, head_size)
    score_scale = 1.0 / math.sqrt(head_size)
    cached = (
        jnp.einsum("rkgd,rtkd->rkgt", qvals, cache_keys, preferred_element_type=jnp.float32)
        * score_scale
    )
    fresh = (
        jnp.einsum("rkgd,rkd->rkg", qvals, new_keys, preferred_element_type=jnp.float32)
        * score_scale
    )
    positions = jnp.arange(slots_cached, dtype=jnp.int32)
    valid = positions[None, :] < lengths[:, None]
    cached = jnp.where(valid[:, None, None, :], cached, jnp.float32(-1e30))
    highest = jnp.maximum(jnp.max(cached, axis=-1), fresh)
    cached_exp = jnp.exp(cached - highest[..., None])
    fresh_exp = jnp.exp(fresh - highest)
    total = jnp.sum(cached_exp, axis=-1) + fresh_exp
    cached_w = (cached_exp / total[..., None]).astype(jnp.bfloat16)
    fresh_w = (fresh_exp / total).astype(jnp.bfloat16)
    result = jnp.einsum(
        "rkgt,rtkd->rkgd", cached_w, cache_values, preferred_element_type=jnp.float32
    )
    result = (
        result
        + fresh_w.astype(jnp.float32)[..., None] * new_values.astype(jnp.float32)[:, :, None, :]
    )
    return result.reshape(count, kv_heads * group * head_size).astype(jnp.bfloat16)


def moe_kernel(
    nk, nz, w,
    out_in, wg_hbm, wu_hbm, wd_hbm, ret_out,
    wg, wu, wd, zin, xall, acc_g, acc_u, hid, po, pr, s, t1, t2, t3, zout, zret,
    w_sem, zs_s, zs_r, p1_s, p1_r, p2_s, p2_r, fw_s, fw_r, dd_s, dd_r,
    ex_s, ex_r, t1_s, t1_r, t2_s, t2_r, t3_s, t3_r, zo_s, zo_r,
):
    g = lax.axis_index("grp")
    xy = lax.axis_index("exp")
    z = lax.axis_index("hid")
    x = xy // SIDE
    y = xy % SIDE
    wide = 4 * w
    bf = jnp.bfloat16
    f32 = jnp.float32

    def at_x(d):
        return (g, ((x + d) % SIDE) * SIDE + y, z)

    def at_y(d):
        return (g, x * SIDE + (y + d) % SIDE, z)

    def at_z(d):
        return (g, xy, (z + d) % nz)

    partner = (1 - g, xy, z)
    along = (at_x, at_y)
    across = (at_y, at_x)

    sent = []

    def send(src, dst, ssem, rsem, dev):
        copy = pltpu.make_async_remote_copy(
            src_ref=src, dst_ref=dst, send_sem=ssem, recv_sem=rsem,
            device_id=dev, device_id_type=MESH,
        )
        copy.start()
        sent.append(copy)

    def landed(dst, ssem, rsem, dev):
        pltpu.make_async_remote_copy(
            src_ref=dst, dst_ref=dst, send_sem=ssem, recv_sem=rsem,
            device_id=dev, device_id_type=MESH,
        ).wait_recv()

    weight_copies = [
        pltpu.make_async_copy(wg_hbm, wg, w_sem.at[0]),
        pltpu.make_async_copy(wu_hbm, wu, w_sem.at[1]),
        pltpu.make_async_copy(wd_hbm, wd, w_sem.at[2]),
    ]
    for copy in weight_copies:
        copy.start()

    barrier = pltpu.get_barrier_semaphore()
    friends = [partner]
    friends += [at_x(d) for d in (1, 2, 3)] + [at_y(d) for d in (1, 2, 3)]
    friends += [at_z(d) for d in range(1, nz)]
    for dev in friends:
        pl.semaphore_signal(barrier, inc=1, device_id=dev, device_id_type=MESH)
    pl.semaphore_wait(barrier, len(friends))

    for k in range(nk):
        for d in range(1, nz):
            to = (z + d) % nz
            send(out_in.at[k, to], zin.at[k, z], zs_s.at[k, d - 1], zs_r.at[k, d - 1], at_z(d))
        zin[k, z] = out_in[k, z]

    units = nz * 16
    row = lax.broadcasted_iota(jnp.int32, (units, units), 0)
    col = lax.broadcasted_iota(jnp.int32, (units, units), 1)
    spread = (col == (row % 16) * 8 + row // 16).astype(bf)
    gather = (row == (col % 16) * 8 + col // 16).astype(bf)

    def mine(k, h, d):
        if h == 0:
            return xall.at[k, 0, g, :, (y + d) % SIDE]
        return xall.at[k, 1, g, (x + d) % SIDE]

    def mine_half(k, h, d, side):
        if h == 0:
            return xall.at[k, 0, g, pl.ds(2 * side, 2), (y + d) % SIDE]
        return xall.at[k, 1, g, (x + d) % SIDE, pl.ds(2 * side, 2)]

    def a0(k):
        for d in range(1, nz):
            src = (z + nz - d) % nz
            landed(zin.at[k, src], zs_s.at[k, d - 1], zs_r.at[k, d - 1], at_z(nz - d))
        block = zin[k].reshape(units, w)
        block = jnp.dot(spread, block, preferred_element_type=f32).astype(bf)
        for part in range(8):
            h, q = part // 4, part % 4
            xall[k, h, g, x, y, :, q * w:(q + 1) * w] = block[part * 16:(part + 1) * 16]
        for h in range(2):
            for d in (1, 3, 2):
                ref = xall.at[k, h, g, x, y]
                send(ref, ref, p1_s.at[k, h, d - 1], p1_r.at[k, h, d - 1], along[h](d))

    def a1(k):
        for h in range(2):
            for d in (1, 3, 2):
                if h == 0:
                    ref = xall.at[k, 0, g, (x + SIDE - d) % SIDE, y]
                else:
                    ref = xall.at[k, 1, g, x, (y + SIDE - d) % SIDE]
                landed(ref, p1_s.at[k, h, d - 1], p1_r.at[k, h, d - 1], along[h](SIDE - d))
            ref = mine(k, h, 0)
            send(ref, ref, p2_s.at[k, h, 0], p2_r.at[k, h, 0], across[h](1))
            send(ref, ref, p2_s.at[k, h, 1], p2_r.at[k, h, 1], across[h](3))
            send(ref, ref, dd_s.at[k, h, 0], dd_r.at[k, h, 0], partner)

    def a2(k):
        for h in range(2):
            for n, d in ((0, 3), (1, 1)):
                ref = mine(k, h, d)
                landed(ref, p2_s.at[k, h, n], p2_r.at[k, h, n], across[h](d))
                half = mine_half(k, h, d, n)
                send(half, half, fw_s.at[k, h, n], fw_r.at[k, h, n], across[h](SIDE - d))
                send(ref, ref, dd_s.at[k, h, d], dd_r.at[k, h, d], partner)

    def a3(k):
        for h in range(2):
            for n, d in ((0, 3), (1, 1)):
                half = mine_half(k, h, 2, n)
                landed(half, fw_s.at[k, h, n], fw_r.at[k, h, n], across[h](d))
            ref = mine(k, h, 2)
            send(ref, ref, dd_s.at[k, h, 2], dd_r.at[k, h, 2], partner)

    def m(k):
        if k == 0:
            weight_copies[0].wait()
            weight_copies[1].wait()
        for h in range(2):
            for d in range(SIDE):
                if h == 0:
                    ref = xall.at[k, 0, 1 - g, :, (y + d) % SIDE]
                else:
                    ref = xall.at[k, 1, 1 - g, (x + d) % SIDE]
                landed(ref, dd_s.at[k, h, d], dd_r.at[k, h, d], partner)
        first = k * 2 * wide

        @pl.loop(0, 2)
        def _(i):
            gate, up = None, None
            for h in range(2):
                lhs = xall[k, h, i].reshape(256, wide)
                rows = slice(first + h * wide, first + (h + 1) * wide)
                a = jnp.dot(lhs, wg[rows, :], preferred_element_type=f32)
                b = jnp.dot(lhs, wu[rows, :], preferred_element_type=f32)
                gate = a if gate is None else gate + a
                up = b if up is None else up + b
            if k > 0:
                gate = gate + acc_g[i]
                up = up + acc_u[i]
            if k < nk - 1:
                acc_g[i] = gate
                acc_u[i] = up
            else:
                hid[i] = (gate * jax.nn.sigmoid(gate) * up).astype(bf)

    def down(k):
        if k == 0:
            weight_copies[2].wait()
        for whose in range(2):
            lhs = hid[(1 - g) if whose == 0 else g]
            for h in range(2):
                cols = slice((2 * k + h) * wide, (2 * k + h + 1) * wide)
                part = jnp.dot(lhs, wd[:, cols], preferred_element_type=f32).astype(bf)
                part = part.reshape(SIDE, SIDE, 16, wide)
                if whose == 0:
                    po[k, h] = part
                    send(po.at[k, h], pr.at[k, h], ex_s.at[k, h], ex_r.at[k, h], partner)
                else:
                    s[k, h] = part

    def add(*terms):
        total = terms[0].astype(f32)
        for term in terms[1:]:
            total = total + term.astype(f32)
        return total.astype(bf)

    def s_block(k, h, d):
        if h == 0:
            return s.at[k, 0, :, (y + d) % SIDE]
        return s.at[k, 1, (x + d) % SIDE]

    def s_half(k, h, d, side):
        if h == 0:
            return s.at[k, 0, pl.ds(2 * side, 2), (y + d) % SIDE]
        return s.at[k, 1, (x + d) % SIDE, pl.ds(2 * side, 2)]

    def s1(k):
        for h in range(2):
            landed(pr.at[k, h], ex_s.at[k, h], ex_r.at[k, h], partner)
            s[k, h] = add(s[k, h], pr[k, h])
            send(s_half(k, h, 2, 0), t1.at[k, h, 0], t1_s.at[k, h, 0], t1_r.at[k, h, 0], across[h](1))
            send(s_half(k, h, 2, 1), t1.at[k, h, 1], t1_s.at[k, h, 1], t1_r.at[k, h, 1], across[h](3))

    def s2(k):
        for h in range(2):
            for n, d in ((0, 1), (1, 3)):
                landed(t1.at[k, h, n], t1_s.at[k, h, n], t1_r.at[k, h, n], across[h](SIDE - d))
                half = s_half(k, h, d, n)
                half[...] = add(half[...], t1[k, h, n])
                send(s_block(k, h, d), t2.at[k, h, n], t2_s.at[k, h, n], t2_r.at[k, h, n], across[h](d))

    def s3(k):
        for h in range(2):
            for n, d in ((0, 1), (1, 3)):
                landed(t2.at[k, h, n], t2_s.at[k, h, n], t2_r.at[k, h, n], across[h](SIDE - d))
            block = s_block(k, h, 0)
            block[...] = add(block[...], t2[k, h, 0], t2[k, h, 1])
            for d in (1, 3, 2):
                if h == 0:
                    src = s.at[k, 0, (x + d) % SIDE, y]
                else:
                    src = s.at[k, 1, x, (y + d) % SIDE]
                send(src, t3.at[k, h, d - 1], t3_s.at[k, h, d - 1], t3_r.at[k, h, d - 1], along[h](d))

    def s4(k):
        parts = []
        for h in range(2):
            for d in (1, 3, 2):
                landed(t3.at[k, h, d - 1], t3_s.at[k, h, d - 1], t3_r.at[k, h, d - 1], along[h](SIDE - d))
            total = add(s[k, h, x, y], t3[k, h, 0], t3[k, h, 1], t3[k, h, 2])
            parts += [total[:, q * w:(q + 1) * w] for q in range(4)]
        block = jnp.concatenate(parts, axis=0)
        block = jnp.dot(gather, block, preferred_element_type=f32).astype(bf)
        zout[k] = block.reshape(nz, 16, w)
        for d in range(1, nz):
            to = (z + d) % nz
            send(zout.at[k, to], zret.at[k, z], zo_s.at[k, d - 1], zo_r.at[k, d - 1], at_z(d))
        zret[k, z] = zout[k, z]

    def s5(k):
        for d in range(1, nz):
            src = (z + nz - d) % nz
            landed(zret.at[k, src], zo_s.at[k, d - 1], zo_r.at[k, d - 1], at_z(nz - d))
        ret_out[k] = zret[k]

    def run(stages):
        for t in range(nk + len(stages) - 1):
            for j, stage in enumerate(stages):
                if 0 <= t - j < nk:
                    stage(t - j)

    run([a0, a1, a2, a3, m])
    run([down, s1, s2, s3, s4, s5])
    for copy in sent:
        copy.wait_send()


def experts(outgoing, w_gate, w_up, w_down, nk):
    nz = outgoing.shape[1]
    w = outgoing.shape[3]
    wide = 4 * w
    width, slice_size = w_gate.shape
    bf = jnp.bfloat16
    dma = pltpu.SemaphoreType.DMA
    vmem = pltpu.VMEM
    blocks = (nk, 2, SIDE, SIDE, 16, wide)
    scratch = [
        vmem((width, slice_size), bf),
        vmem((width, slice_size), bf),
        vmem((slice_size, width), bf),
        vmem((nk, nz, 16, w), bf),
        vmem((nk, 2, 2, SIDE, SIDE, 16, wide), bf),
        vmem((2, 256, slice_size), jnp.float32),
        vmem((2, 256, slice_size), jnp.float32),
        vmem((2, 256, slice_size), bf),
        vmem(blocks, bf),
        vmem(blocks, bf),
        vmem(blocks, bf),
        vmem((nk, 2, 2, 2, 16, wide), bf),
        vmem((nk, 2, 2, 4, 16, wide), bf),
        vmem((nk, 2, 3, 16, wide), bf),
        vmem((nk, nz, 16, w), bf),
        vmem((nk, nz, 16, w), bf),
        dma((3,)),
    ]
    for shape in [(nk, nz - 1), (nk, 2, 3), (nk, 2, 2), (nk, 2, 2), (nk, 2, 4),
                  (nk, 2), (nk, 2, 2), (nk, 2, 2), (nk, 2, 3), (nk, nz - 1)]:
        scratch += [dma(shape), dma(shape)]
    any_spec = pl.BlockSpec(memory_space=pl.ANY)
    return pl.pallas_call(
        functools.partial(moe_kernel, nk, nz, w),
        out_shape=jax.ShapeDtypeStruct(outgoing.shape, bf),
        in_specs=[pl.BlockSpec(memory_space=pltpu.VMEM), any_spec, any_spec, any_spec],
        out_specs=pl.BlockSpec(memory_space=pltpu.VMEM),
        scratch_shapes=scratch,
        compiler_params=pltpu.CompilerParams(
            collective_id=0, has_side_effects=True, vmem_limit_bytes=48 * 1024 * 1024
        ),
    )(outgoing, w_gate, w_up, w_down)


def per_device(
    queries,
    cache_keys,
    cache_values,
    new_keys,
    new_values,
    lengths,
    residual,
    norm_gain,
    routes,
    gate_logits,
    w_gate,
    w_up,
    w_down,
):
    attended = attend(queries, cache_keys, cache_values, new_keys, new_values, lengths)
    mixed = residual.astype(jnp.float32) + attended.astype(jnp.float32)
    normed = (
        mixed * lax.rsqrt(jnp.mean(mixed * mixed, axis=-1, keepdims=True) + 1e-05) * norm_gain
    ).astype(jnp.bfloat16)
    nz = lax.axis_size("hid")
    width = normed.shape[1]
    nk = 3
    w = width // (8 * nk)
    expert_ids = jnp.arange(nz, dtype=jnp.int32)
    chosen = routes[:, :, None] == expert_ids[None, None, :]
    gates = jax.nn.softmax(gate_logits, axis=-1)
    combine = jnp.sum(jnp.where(chosen, gates[:, :, None], jnp.float32(0.0)), axis=1)
    selected = jnp.any(chosen, axis=1).astype(jnp.int32)
    ranking = jnp.cumsum(selected, axis=0) - selected
    slot_ids = jnp.arange(CAP, dtype=jnp.int32)
    placement = (selected.T[:, None, :] == 1) & (ranking.T[:, None, :] == slot_ids[None, :, None])
    outgoing = jnp.einsum(
        "ecr,rd->ecd", placement.astype(jnp.bfloat16), normed, preferred_element_type=jnp.float32
    ).astype(jnp.bfloat16)
    outgoing = outgoing.reshape(nz, CAP, nk, 8, w).transpose(2, 0, 1, 3, 4).reshape(nk, nz, 16, w)
    returned = experts(outgoing, w_gate[0], w_up[0], w_down[0], nk)
    returned = returned.reshape(nk, nz, CAP, 8, w).transpose(1, 2, 0, 3, 4).reshape(nz, CAP, width)
    mixing = placement.astype(jnp.float32) * combine.T[:, None, :]
    moe = jnp.einsum("ecr,ecd->rd", mixing, returned.astype(jnp.float32))
    return (mixed + moe).astype(jnp.bfloat16)


def solution(mesh):
    in_specs = (
        P(("grp", "exp", "hid"), None, None),
        P(("grp", "exp", "hid"), None, None, None),
        P(("grp", "exp", "hid"), None, None, None),
        P(("grp", "exp", "hid"), None, None),
        P(("grp", "exp", "hid"), None, None),
        P(("grp", "exp", "hid")),
        P(("grp", "exp", "hid"), None),
        P(),
        P(("grp", "exp", "hid"), None),
        P(("grp", "exp", "hid"), None),
        P("hid", None, ("grp", "exp")),
        P("hid", None, ("grp", "exp")),
        P("hid", ("grp", "exp"), None),
    )
    out_specs = P(("grp", "exp", "hid"), None)
    return jax.shard_map(
        per_device, mesh=mesh, in_specs=in_specs, out_specs=out_specs, check_vma=False
    )
```

```python
import functools
import math

import jax
import jax.numpy as jnp
from jax import lax
from jax.experimental import pallas as pl
from jax.experimental.pallas import tpu as pltpu
from jax.sharding import PartitionSpec as P

CAP = 2
SIDE = 4
MESH = pl.DeviceIdType.MESH


def attend(queries, cache_keys, cache_values, new_keys, new_values, lengths):
    count = queries.shape[0]
    kv_heads = cache_keys.shape[2]
    head_size = cache_keys.shape[3]
    slots_cached = cache_keys.shape[1]
    group = queries.shape[1] // kv_heads
    qvals = queries.reshape(count, kv_heads, group, head_size)
    score_scale = 1.0 / math.sqrt(head_size)
    cached = (
        jnp.einsum("rkgd,rtkd->rkgt", qvals, cache_keys, preferred_element_type=jnp.float32)
        * score_scale
    )
    fresh = (
        jnp.einsum("rkgd,rkd->rkg", qvals, new_keys, preferred_element_type=jnp.float32)
        * score_scale
    )
    positions = jnp.arange(slots_cached, dtype=jnp.int32)
    valid = positions[None, :] < lengths[:, None]
    cached = jnp.where(valid[:, None, None, :], cached, jnp.float32(-1e30))
    highest = jnp.maximum(jnp.max(cached, axis=-1), fresh)
    cached_exp = jnp.exp(cached - highest[..., None])
    fresh_exp = jnp.exp(fresh - highest)
    total = jnp.sum(cached_exp, axis=-1) + fresh_exp
    cached_w = (cached_exp / total[..., None]).astype(jnp.bfloat16)
    fresh_w = (fresh_exp / total).astype(jnp.bfloat16)
    result = jnp.einsum(
        "rkgt,rtkd->rkgd", cached_w, cache_values, preferred_element_type=jnp.float32
    )
    result = (
        result
        + fresh_w.astype(jnp.float32)[..., None] * new_values.astype(jnp.float32)[:, :, None, :]
    )
    return result.reshape(count, kv_heads * group * head_size).astype(jnp.bfloat16)


def moe_kernel(ws, nz, *refs):
    bf = jnp.bfloat16
    f32 = jnp.float32
    nk = len(ws)
    chunks = range(nk)
    starts = [8 * sum(ws[:k]) for k in chunks]
    refs = list(refs)
    lanes = [pl.ds(start // 8, w) for start, w in zip(starts, ws)]

    def take(n):
        got = refs[:n]
        del refs[:n]
        return got

    out_in, wg_hbm, wu_hbm, wd_hbm, ret_out = take(5)
    wg, wu, wd, acc_g, acc_u, hid = take(6)
    zin, xall, po, pr, part, t1, t2, t3, zout, zret = [take(nk) for _ in range(10)]
    (w_sem, zs_s, zs_r, p1_s, p1_r, p2_s, p2_r, fw_s, fw_r, dd_s, dd_r,
     ex_s, ex_r, t1_s, t1_r, t2_s, t2_r, t3_s, t3_r, zo_s, zo_r) = refs

    g = lax.axis_index("grp")
    xy = lax.axis_index("exp")
    z = lax.axis_index("hid")
    x = xy // SIDE
    y = xy % SIDE

    def at_x(d):
        return (g, ((x + d) % SIDE) * SIDE + y, z)

    def at_y(d):
        return (g, x * SIDE + (y + d) % SIDE, z)

    def at_z(d):
        return (g, xy, (z + d) % nz)

    partner = (1 - g, xy, z)
    along = (at_x, at_y)
    across = (at_y, at_x)
    far_first = (2, 1, 3)
    z_far_first = sorted(range(1, nz), key=lambda d: -min(d, nz - d))

    sent = []

    def send(src, dst, ssem, rsem, dev):
        copy = pltpu.make_async_remote_copy(
            src_ref=src, dst_ref=dst, send_sem=ssem, recv_sem=rsem,
            device_id=dev, device_id_type=MESH,
        )
        copy.start()
        sent.append(copy)

    def landed(dst, ssem, rsem, dev):
        pltpu.make_async_remote_copy(
            src_ref=dst, dst_ref=dst, send_sem=ssem, recv_sem=rsem,
            device_id=dev, device_id_type=MESH,
        ).wait_recv()

    barrier = pltpu.get_barrier_semaphore()
    friends = [partner]
    friends += [at_x(d) for d in (1, 2, 3)] + [at_y(d) for d in (1, 2, 3)]
    friends += [at_z(d) for d in range(1, nz)]
    for dev in friends:
        pl.semaphore_signal(barrier, inc=1, device_id=dev, device_id_type=MESH)
    weight_copies = [
        pltpu.make_async_copy(wg_hbm, wg, w_sem.at[0]),
        pltpu.make_async_copy(wu_hbm, wu, w_sem.at[1]),
        pltpu.make_async_copy(wd_hbm, wd, w_sem.at[2]),
    ]
    for copy in weight_copies:
        copy.start()
    pl.semaphore_wait(barrier, len(friends))

    for k in chunks:
        for d in z_far_first:
            to = (z + d) % nz
            send(out_in.at[to, :, lanes[k]], zin[k].at[z], zs_s.at[k, d - 1], zs_r.at[k, d - 1], at_z(d))
    for k in chunks:
        zin[k][z] = out_in[z, :, lanes[k]]

    units = nz * 16
    row = lax.broadcasted_iota(jnp.int32, (units, units), 0)
    col = lax.broadcasted_iota(jnp.int32, (units, units), 1)
    spread = (col == (row % 16) * 8 + row // 16).astype(bf)
    gather = (row == (col % 16) * 8 + col // 16).astype(bf)

    def mine(k, h, d):
        if h == 0:
            return xall[k].at[0, g, :, (y + d) % SIDE]
        return xall[k].at[1, g, (x + d) % SIDE]

    def mine_half(k, h, d, side):
        if h == 0:
            return xall[k].at[0, g, pl.ds(2 * side, 2), (y + d) % SIDE]
        return xall[k].at[1, g, (x + d) % SIDE, pl.ds(2 * side, 2)]

    def a0(k):
        w = ws[k]
        for d in z_far_first[::-1]:
            src = (z + nz - d) % nz
            landed(zin[k].at[src], zs_s.at[k, d - 1], zs_r.at[k, d - 1], at_z(nz - d))
        block = zin[k][...].reshape(units, w)
        block = jnp.dot(spread, block, preferred_element_type=f32).astype(bf)
        for n in range(8):
            h, q = n // 4, n % 4
            xall[k][h, g, x, y, :, q * w:(q + 1) * w] = block[n * 16:(n + 1) * 16]
        for h in range(2):
            for d in far_first:
                ref = xall[k].at[h, g, x, y]
                send(ref, ref, p1_s.at[k, h, d - 1], p1_r.at[k, h, d - 1], along[h](d))

    def a1(k):
        for h in range(2):
            for d in far_first:
                if h == 0:
                    ref = xall[k].at[0, g, (x + SIDE - d) % SIDE, y]
                else:
                    ref = xall[k].at[1, g, x, (y + SIDE - d) % SIDE]
                landed(ref, p1_s.at[k, h, d - 1], p1_r.at[k, h, d - 1], along[h](SIDE - d))
            ref = mine(k, h, 0)
            send(ref, ref, p2_s.at[k, h, 0], p2_r.at[k, h, 0], across[h](1))
            send(ref, ref, p2_s.at[k, h, 1], p2_r.at[k, h, 1], across[h](3))
            send(ref, ref, dd_s.at[k, h, 0], dd_r.at[k, h, 0], partner)

    def a2(k):
        for h in range(2):
            for n, d in ((0, 3), (1, 1)):
                ref = mine(k, h, d)
                landed(ref, p2_s.at[k, h, n], p2_r.at[k, h, n], across[h](d))
                half = mine_half(k, h, d, n)
                send(half, half, fw_s.at[k, h, n], fw_r.at[k, h, n], across[h](SIDE - d))
                send(ref, ref, dd_s.at[k, h, d], dd_r.at[k, h, d], partner)

    def a3(k):
        for h in range(2):
            for n, d in ((0, 3), (1, 1)):
                half = mine_half(k, h, 2, n)
                landed(half, fw_s.at[k, h, n], fw_r.at[k, h, n], across[h](d))
            ref = mine(k, h, 2)
            send(ref, ref, dd_s.at[k, h, 2], dd_r.at[k, h, 2], partner)

    def m(k):
        wide = 4 * ws[k]
        if k == 0:
            weight_copies[0].wait()
            weight_copies[1].wait()
        for h in range(2):
            for d in range(SIDE):
                if h == 0:
                    ref = xall[k].at[0, 1 - g, :, (y + d) % SIDE]
                else:
                    ref = xall[k].at[1, 1 - g, (x + d) % SIDE]
                landed(ref, dd_s.at[k, h, d], dd_r.at[k, h, d], partner)

        @pl.loop(0, 2)
        def _(i):
            gate, up = None, None
            for h in range(2):
                lhs = xall[k][h, i].reshape(256, wide)
                rows = slice(starts[k] + h * wide, starts[k] + (h + 1) * wide)
                a = jnp.dot(lhs, wg[rows, :], preferred_element_type=f32)
                b = jnp.dot(lhs, wu[rows, :], preferred_element_type=f32)
                gate = a if gate is None else gate + a
                up = b if up is None else up + b
            if k > 0:
                gate = gate + acc_g[i]
                up = up + acc_u[i]
            if k < nk - 1:
                acc_g[i] = gate
                acc_u[i] = up
            else:
                hid[i] = (gate * jax.nn.sigmoid(gate) * up).astype(bf)

    def down(k):
        wide = 4 * ws[k]
        if k == 0:
            weight_copies[2].wait()
        for whose in range(2):
            lhs = hid[(1 - g) if whose == 0 else g]
            for h in range(2):
                cols = slice(starts[k] + h * wide, starts[k] + (h + 1) * wide)
                value = jnp.dot(lhs, wd[:, cols], preferred_element_type=f32).astype(bf)
                value = value.reshape(SIDE, SIDE, 16, wide)
                if whose == 0:
                    po[k][h] = value
                    send(po[k].at[h], pr[k].at[h], ex_s.at[k, h], ex_r.at[k, h], partner)
                else:
                    part[k][h] = value

    def total(*terms):
        value = terms[0][...].astype(f32)
        for term in terms[1:]:
            value = value + term[...].astype(f32)
        return value.astype(bf)

    def block_of(buf, k, h, d):
        if h == 0:
            return buf[k].at[0, :, (y + d) % SIDE]
        return buf[k].at[1, (x + d) % SIDE]

    def half_of(buf, k, h, d, side):
        if h == 0:
            return buf[k].at[0, pl.ds(2 * side, 2), (y + d) % SIDE]
        return buf[k].at[1, (x + d) % SIDE, pl.ds(2 * side, 2)]

    def s1(k):
        for h in range(2):
            landed(pr[k].at[h], ex_s.at[k, h], ex_r.at[k, h], partner)
            block = block_of(part, k, h, 2)
            block[...] = total(block, block_of(pr, k, h, 2))
            for n, d in ((0, 1), (1, 3)):
                send(half_of(part, k, h, 2, n), t1[k].at[h, n], t1_s.at[k, h, n], t1_r.at[k, h, n], across[h](d))

    def s2(k):
        for h in range(2):
            for n, d in ((0, 1), (1, 3)):
                rest = half_of(part, k, h, d, 1 - n)
                rest[...] = total(rest, half_of(pr, k, h, d, 1 - n))
                landed(t1[k].at[h, n], t1_s.at[k, h, n], t1_r.at[k, h, n], across[h](SIDE - d))
                half = half_of(part, k, h, d, n)
                half[...] = total(half, half_of(pr, k, h, d, n), t1[k].at[h, n])
                send(block_of(part, k, h, d), t2[k].at[h, n], t2_s.at[k, h, n], t2_r.at[k, h, n], across[h](d))

    def s3(k):
        for h in range(2):
            for n, d in ((0, 1), (1, 3)):
                landed(t2[k].at[h, n], t2_s.at[k, h, n], t2_r.at[k, h, n], across[h](SIDE - d))
            block = block_of(part, k, h, 0)
            block[...] = total(block, block_of(pr, k, h, 0), t2[k].at[h, 0], t2[k].at[h, 1])
            for d in far_first:
                if h == 0:
                    src = part[k].at[0, (x + d) % SIDE, y]
                else:
                    src = part[k].at[1, x, (y + d) % SIDE]
                send(src, t3[k].at[h, d - 1], t3_s.at[k, h, d - 1], t3_r.at[k, h, d - 1], along[h](d))

    def s4(k):
        w = ws[k]
        parts = []
        for h in range(2):
            for d in far_first[::-1]:
                landed(t3[k].at[h, d - 1], t3_s.at[k, h, d - 1], t3_r.at[k, h, d - 1], along[h](SIDE - d))
            value = total(part[k].at[h, x, y], *[t3[k].at[h, n] for n in range(3)])
            parts += [value[:, q * w:(q + 1) * w] for q in range(4)]
        block = jnp.concatenate(parts, axis=0)
        block = jnp.dot(gather, block, preferred_element_type=f32).astype(bf)
        zout[k][...] = block.reshape(nz, 16, w)
        for d in z_far_first:
            to = (z + d) % nz
            send(zout[k].at[to], zret[k].at[z], zo_s.at[k, d - 1], zo_r.at[k, d - 1], at_z(d))
        zret[k][z] = zout[k][z]

    def s5(k):
        for d in z_far_first[::-1]:
            src = (z + nz - d) % nz
            landed(zret[k].at[src], zo_s.at[k, d - 1], zo_r.at[k, d - 1], at_z(nz - d))
        ret_out[:, :, lanes[k]] = zret[k][...]

    for stage in (a0, a1, a2):
        for k in chunks:
            stage(k)
    for k in range(nk + 1):
        if k < nk:
            a3(k)
        if k > 0:
            m(k - 1)
    for k in range(nk + 1):
        if k < nk:
            down(k)
        if k > 0:
            s1(k - 1)
    for stage in (s2, s3, s4, s5):
        for k in chunks:
            stage(k)
    for copy in sent:
        copy.wait_send()


def experts(outgoing, w_gate, w_up, w_down, ws):
    nz = outgoing.shape[0]
    nk = len(ws)
    width, slice_size = w_gate.shape
    bf = jnp.bfloat16
    dma = pltpu.SemaphoreType.DMA
    vmem = pltpu.VMEM
    scratch = [
        vmem((width, slice_size), bf),
        vmem((width, slice_size), bf),
        vmem((slice_size, width), bf),
        vmem((2, 256, slice_size), jnp.float32),
        vmem((2, 256, slice_size), jnp.float32),
        vmem((2, 256, slice_size), bf),
    ]
    blocks = (2, SIDE, SIDE, 16)
    for lead in ((nz, 16), (2,) + blocks, blocks, blocks, blocks, (2, 2, 2, 16), (2, 2, 4, 16),
                 (2, 3, 16), (nz, 16), (nz, 16)):
        scratch += [vmem(lead + ((w if lead[0] == nz else 4 * w),), bf) for w in ws]
    scratch.append(dma((3,)))
    for shape in [(nk, nz - 1), (nk, 2, 3), (nk, 2, 2), (nk, 2, 2), (nk, 2, 4),
                  (nk, 2), (nk, 2, 2), (nk, 2, 2), (nk, 2, 3), (nk, nz - 1)]:
        scratch += [dma(shape), dma(shape)]
    any_spec = pl.BlockSpec(memory_space=pl.ANY)
    vmem_spec = pl.BlockSpec(memory_space=pltpu.VMEM)
    return pl.pallas_call(
        functools.partial(moe_kernel, ws, nz),
        out_shape=jax.ShapeDtypeStruct(outgoing.shape, bf),
        in_specs=[vmem_spec] + [any_spec] * 3,
        out_specs=vmem_spec,
        scratch_shapes=scratch,
        compiler_params=pltpu.CompilerParams(
            collective_id=0, has_side_effects=True, vmem_limit_bytes=48 * 1024 * 1024
        ),
    )(outgoing, w_gate, w_up, w_down)


def per_device(
    queries,
    cache_keys,
    cache_values,
    new_keys,
    new_values,
    lengths,
    residual,
    norm_gain,
    routes,
    gate_logits,
    w_gate,
    w_up,
    w_down,
):
    attended = attend(queries, cache_keys, cache_values, new_keys, new_values, lengths)
    mixed = residual.astype(jnp.float32) + attended.astype(jnp.float32)
    normed = (
        mixed * lax.rsqrt(jnp.mean(mixed * mixed, axis=-1, keepdims=True) + 1e-05) * norm_gain
    ).astype(jnp.bfloat16)
    nz = lax.axis_size("hid")
    width = normed.shape[1]
    ws = (256, 256, 256)
    expert_ids = jnp.arange(nz, dtype=jnp.int32)
    chosen = routes[:, :, None] == expert_ids[None, None, :]
    gates = jax.nn.softmax(gate_logits, axis=-1)
    combine = jnp.sum(jnp.where(chosen, gates[:, :, None], jnp.float32(0.0)), axis=1)
    selected = jnp.any(chosen, axis=1).astype(jnp.int32)
    ranking = jnp.cumsum(selected, axis=0) - selected
    slot_ids = jnp.arange(CAP, dtype=jnp.int32)
    placement = (selected.T[:, None, :] == 1) & (ranking.T[:, None, :] == slot_ids[None, :, None])
    outgoing = jnp.einsum(
        "ecr,rd->ecd", placement.astype(jnp.bfloat16), normed, preferred_element_type=jnp.float32
    ).astype(jnp.bfloat16)
    ends = [8 * sum(ws[: k + 1]) for k in range(len(ws))]
    outgoing = jnp.concatenate(
        [outgoing[:, :, end - 8 * w:end].reshape(nz, CAP * 8, w) for end, w in zip(ends, ws)],
        axis=-1,
    )
    returned = experts(outgoing, w_gate[0], w_up[0], w_down[0], ws)
    returned = jnp.concatenate(
        [
            returned[:, :, end // 8 - w:end // 8].reshape(nz, CAP, 8 * w)
            for end, w in zip(ends, ws)
        ],
        axis=-1,
    )
    mixing = placement.astype(jnp.float32) * combine.T[:, None, :]
    moe = jnp.einsum("ecr,ecd->rd", mixing, returned.astype(jnp.float32))
    return (mixed + moe).astype(jnp.bfloat16)


def solution(mesh):
    in_specs = (
        P(("grp", "exp", "hid"), None, None),
        P(("grp", "exp", "hid"), None, None, None),
        P(("grp", "exp", "hid"), None, None, None),
        P(("grp", "exp", "hid"), None, None),
        P(("grp", "exp", "hid"), None, None),
        P(("grp", "exp", "hid")),
        P(("grp", "exp", "hid"), None),
        P(),
        P(("grp", "exp", "hid"), None),
        P(("grp", "exp", "hid"), None),
        P("hid", None, ("grp", "exp")),
        P("hid", None, ("grp", "exp")),
        P("hid", ("grp", "exp"), None),
    )
    out_specs = P(("grp", "exp", "hid"), None)
    return jax.shard_map(
        per_device, mesh=mesh, in_specs=in_specs, out_specs=out_specs, check_vma=False
    )
```

```python
import functools
import math

import jax
import jax.numpy as jnp
from jax import lax
from jax.experimental import pallas as pl
from jax.experimental.pallas import tpu as pltpu
from jax.sharding import PartitionSpec as P

CAP = 2
SIDE = 4
MESH = pl.DeviceIdType.MESH


def attend(queries, cache_keys, cache_values, new_keys, new_values, lengths):
    count = queries.shape[0]
    kv_heads = cache_keys.shape[2]
    head_size = cache_keys.shape[3]
    slots_cached = cache_keys.shape[1]
    group = queries.shape[1] // kv_heads
    qvals = queries.reshape(count, kv_heads, group, head_size)
    score_scale = 1.0 / math.sqrt(head_size)
    cached = (
        jnp.einsum("rkgd,rtkd->rkgt", qvals, cache_keys, preferred_element_type=jnp.float32)
        * score_scale
    )
    fresh = (
        jnp.einsum("rkgd,rkd->rkg", qvals, new_keys, preferred_element_type=jnp.float32)
        * score_scale
    )
    positions = jnp.arange(slots_cached, dtype=jnp.int32)
    valid = positions[None, :] < lengths[:, None]
    cached = jnp.where(valid[:, None, None, :], cached, jnp.float32(-1e30))
    highest = jnp.maximum(jnp.max(cached, axis=-1), fresh)
    cached_exp = jnp.exp(cached - highest[..., None])
    fresh_exp = jnp.exp(fresh - highest)
    total = jnp.sum(cached_exp, axis=-1) + fresh_exp
    cached_w = (cached_exp / total[..., None]).astype(jnp.bfloat16)
    fresh_w = (fresh_exp / total).astype(jnp.bfloat16)
    result = jnp.einsum(
        "rkgt,rtkd->rkgd", cached_w, cache_values, preferred_element_type=jnp.float32
    )
    result = (
        result
        + fresh_w.astype(jnp.float32)[..., None] * new_values.astype(jnp.float32)[:, :, None, :]
    )
    return result.reshape(count, kv_heads * group * head_size).astype(jnp.bfloat16)


def moe_kernel(ws, nz, *refs):
    bf = jnp.bfloat16
    f32 = jnp.float32
    nk = len(ws)
    chunks = range(nk)
    starts = [8 * sum(ws[:k]) for k in chunks]
    refs = list(refs)
    lanes = [pl.ds(start // 8, w) for start, w in zip(starts, ws)]

    def take(n):
        got = refs[:n]
        del refs[:n]
        return got

    out_in, wg_hbm, wu_hbm, wd_hbm, ret_out = take(5)
    wg, wu, wd, acc_g, acc_u, hid = take(6)
    zin, xall, part, t1, t2, t3, zout, zret = [take(nk) for _ in range(8)]
    (w_sem, zs_s, zs_r, p1_s, p1_r, p2_s, p2_r, fw_s, fw_r,
     ws_s, ws_r, t1_s, t1_r, tf_s, tf_r, t2_s, t2_r, t3_s, t3_r, zo_s, zo_r) = refs

    g = lax.axis_index("grp")
    xy = lax.axis_index("exp")
    z = lax.axis_index("hid")
    x = xy // SIDE
    y = xy % SIDE

    def at_x(d):
        return (g, ((x + d) % SIDE) * SIDE + y, z)

    def at_y(d):
        return (g, x * SIDE + (y + d) % SIDE, z)

    def at_z(d):
        return (g, xy, (z + d) % nz)

    partner = (1 - g, xy, z)
    along = (at_x, at_y)
    across = (at_y, at_x)
    far_first = (2, 1, 3)
    z_far_first = sorted(range(1, nz), key=lambda d: -min(d, nz - d))

    sent = []

    def send(src, dst, ssem, rsem, dev):
        copy = pltpu.make_async_remote_copy(
            src_ref=src, dst_ref=dst, send_sem=ssem, recv_sem=rsem,
            device_id=dev, device_id_type=MESH,
        )
        copy.start()
        sent.append(copy)

    def landed(dst, ssem, rsem, dev):
        pltpu.make_async_remote_copy(
            src_ref=dst, dst_ref=dst, send_sem=ssem, recv_sem=rsem,
            device_id=dev, device_id_type=MESH,
        ).wait_recv()

    barrier = pltpu.get_barrier_semaphore()
    friends = [partner]
    friends += [at_x(d) for d in (1, 2, 3)] + [at_y(d) for d in (1, 2, 3)]
    friends += [at_z(d) for d in range(1, nz)]
    for dev in friends:
        pl.semaphore_signal(barrier, inc=1, device_id=dev, device_id_type=MESH)
    weights = ((wg_hbm, wg), (wu_hbm, wu), (wd_hbm, wd))
    own_weights = [
        pltpu.make_async_copy(src, dst.at[g], w_sem.at[n]) for n, (src, dst) in enumerate(weights)
    ]
    for copy in own_weights:
        copy.start()
    pl.semaphore_wait(barrier, len(friends))

    for k in chunks:
        for d in z_far_first:
            to = (z + d) % nz
            send(out_in.at[to, :, lanes[k]], zin[k].at[z], zs_s.at[k, d - 1], zs_r.at[k, d - 1], at_z(d))
    for k in chunks:
        zin[k][z] = out_in[z, :, lanes[k]]
    for n, (src, dst) in enumerate(weights):
        send(src, dst.at[g], ws_s.at[n], ws_r.at[n], partner)

    def ready(n):
        dst = weights[n][1]
        own_weights[n].wait()
        landed(dst.at[1 - g], ws_s.at[n], ws_r.at[n], partner)

    units = nz * 16
    row = lax.broadcasted_iota(jnp.int32, (units, units), 0)
    col = lax.broadcasted_iota(jnp.int32, (units, units), 1)
    spread = (col == (row % 16) * 8 + row // 16).astype(bf)
    gather = (row == (col % 16) * 8 + col // 16).astype(bf)

    def mine_half(k, h, d, side):
        if h == 0:
            return xall[k].at[0, pl.ds(2 * side, 2), (y + d) % SIDE]
        return xall[k].at[1, (x + d) % SIDE, pl.ds(2 * side, 2)]

    def came(k, h, j, d):
        if h == 0:
            return xall[k].at[0, (x + SIDE - j) % SIDE, (y + d) % SIDE]
        return xall[k].at[1, (x + d) % SIDE, (y + SIDE - j) % SIDE]

    def pass_on(k, h, j):
        ref = came(k, h, j, 0)
        for n, d in ((0, 1), (1, 3)):
            send(ref, ref, p2_s.at[k, h, n, j], p2_r.at[k, h, n, j], across[h](d))

    def a0(k):
        w = ws[k]
        for d in z_far_first[::-1]:
            src = (z + nz - d) % nz
            landed(zin[k].at[src], zs_s.at[k, d - 1], zs_r.at[k, d - 1], at_z(nz - d))
        block = zin[k][...].reshape(units, w)
        block = jnp.dot(spread, block, preferred_element_type=f32).astype(bf)
        for n in range(8):
            h, q = n // 4, n % 4
            xall[k][h, x, y, :, q * w:(q + 1) * w] = block[n * 16:(n + 1) * 16]
        for h in range(2):
            for d in far_first:
                ref = xall[k].at[h, x, y]
                send(ref, ref, p1_s.at[k, h, d - 1], p1_r.at[k, h, d - 1], along[h](d))
        for h in range(2):
            pass_on(k, h, 0)

    def a1(k):
        for h in range(2):
            for d in (1, 3, 2):
                ref = came(k, h, d, 0)
                landed(ref, p1_s.at[k, h, d - 1], p1_r.at[k, h, d - 1], along[h](SIDE - d))
                pass_on(k, h, d)

    def a2(k):
        for h in range(2):
            for n, d in ((0, 3), (1, 1)):
                for j in (0, 1, 3, 2):
                    ref = came(k, h, j, d)
                    landed(ref, p2_s.at[k, h, n, j], p2_r.at[k, h, n, j], across[h](d))
                half = mine_half(k, h, d, n)
                send(half, half, fw_s.at[k, h, n], fw_r.at[k, h, n], across[h](SIDE - d))

    def a3(k):
        for h in range(2):
            for n, d in ((0, 3), (1, 1)):
                half = mine_half(k, h, 2, n)
                landed(half, fw_s.at[k, h, n], fw_r.at[k, h, n], across[h](d))

    def m(k):
        wide = 4 * ws[k]
        if k == 0:
            ready(0)
            ready(1)

        @pl.loop(0, 2)
        def _(i):
            gate, up = None, None
            for h in range(2):
                lhs = xall[k][h].reshape(256, wide)
                rows = slice(starts[k] + h * wide, starts[k] + (h + 1) * wide)
                a = jnp.dot(lhs, wg[i, rows, :], preferred_element_type=f32)
                b = jnp.dot(lhs, wu[i, rows, :], preferred_element_type=f32)
                gate = a if gate is None else gate + a
                up = b if up is None else up + b
            if k > 0:
                gate = gate + acc_g[i]
                up = up + acc_u[i]
            if k < nk - 1:
                acc_g[i] = gate
                acc_u[i] = up
            else:
                hid[i] = (gate * jax.nn.sigmoid(gate) * up).astype(bf)

    def down(k, h):
        wide = 4 * ws[k]
        cols = slice(starts[k] + h * wide, starts[k] + (h + 1) * wide)
        value = jnp.dot(hid[0], wd[0, :, cols], preferred_element_type=f32)
        value = value + jnp.dot(hid[1], wd[1, :, cols], preferred_element_type=f32)
        part[k][h] = value.astype(bf).reshape(SIDE, SIDE, 16, wide)

    def total(*terms):
        value = terms[0][...].astype(f32)
        for term in terms[1:]:
            value = value + term[...].astype(f32)
        return value.astype(bf)

    def block_of(buf, k, h, d):
        if h == 0:
            return buf[k].at[0, :, (y + d) % SIDE]
        return buf[k].at[1, (x + d) % SIDE]

    def half_of(buf, k, h, d, side):
        if h == 0:
            return buf[k].at[0, pl.ds(2 * side, 2), (y + d) % SIDE]
        return buf[k].at[1, (x + d) % SIDE, pl.ds(2 * side, 2)]

    def s1(k):
        if k == 0:
            ready(2)
        for h in range(2):
            down(k, h)
            for n, d in ((0, 1), (1, 3)):
                send(half_of(part, k, h, 2, n), t1[k].at[h, n], t1_s.at[k, h, n], t1_r.at[k, h, n], across[h](d))
            for n, d in ((0, 1), (1, 3)):
                send(half_of(part, k, h, d, 1 - n), t2[k].at[h, n, pl.ds(2 * (1 - n), 2)], tf_s.at[k, h, n], tf_r.at[k, h, n], across[h](d))

    def s2(k):
        for h in range(2):
            for n, d in ((0, 1), (1, 3)):
                landed(t1[k].at[h, n], t1_s.at[k, h, n], t1_r.at[k, h, n], across[h](SIDE - d))
                half = half_of(part, k, h, d, n)
                half[...] = total(half, t1[k].at[h, n])
                send(half, t2[k].at[h, n, pl.ds(2 * n, 2)], t2_s.at[k, h, n], t2_r.at[k, h, n], across[h](d))

    def s3(k):
        for h in range(2):
            for n, d in ((0, 1), (1, 3)):
                free = t2[k].at[h, n, pl.ds(2 * (1 - n), 2)]
                landed(free, tf_s.at[k, h, n], tf_r.at[k, h, n], across[h](SIDE - d))
                half = t2[k].at[h, n, pl.ds(2 * n, 2)]
                landed(half, t2_s.at[k, h, n], t2_r.at[k, h, n], across[h](SIDE - d))
            block = block_of(part, k, h, 0)
            block[...] = total(block, t2[k].at[h, 0], t2[k].at[h, 1])
            for d in far_first:
                if h == 0:
                    src = part[k].at[0, (x + d) % SIDE, y]
                else:
                    src = part[k].at[1, x, (y + d) % SIDE]
                send(src, t3[k].at[h, d - 1], t3_s.at[k, h, d - 1], t3_r.at[k, h, d - 1], along[h](d))

    def s4(k):
        w = ws[k]
        parts = []
        for h in range(2):
            for d in far_first[::-1]:
                landed(t3[k].at[h, d - 1], t3_s.at[k, h, d - 1], t3_r.at[k, h, d - 1], along[h](SIDE - d))
            value = total(part[k].at[h, x, y], *[t3[k].at[h, n] for n in range(3)])
            parts += [value[:, q * w:(q + 1) * w] for q in range(4)]
        block = jnp.concatenate(parts, axis=0)
        block = jnp.dot(gather, block, preferred_element_type=f32).astype(bf)
        zout[k][...] = block.reshape(nz, 16, w)
        for d in z_far_first:
            to = (z + d) % nz
            send(zout[k].at[to], zret[k].at[z], zo_s.at[k, d - 1], zo_r.at[k, d - 1], at_z(d))
        zret[k][z] = zout[k][z]

    def s5(k):
        for d in z_far_first[::-1]:
            src = (z + nz - d) % nz
            landed(zret[k].at[src], zo_s.at[k, d - 1], zo_r.at[k, d - 1], at_z(nz - d))
        ret_out[:, :, lanes[k]] = zret[k][...]

    for stage in (a0, a1, a2):
        for k in chunks:
            stage(k)
    for k in chunks:
        a3(k)
        m(k)
    for stage in (s1, s2, s3, s4, s5):
        for k in chunks:
            stage(k)
    for copy in sent:
        copy.wait_send()


def experts(outgoing, w_gate, w_up, w_down, ws):
    nz = outgoing.shape[0]
    nk = len(ws)
    width, slice_size = w_gate.shape
    bf = jnp.bfloat16
    dma = pltpu.SemaphoreType.DMA
    vmem = pltpu.VMEM
    scratch = [
        vmem((2, width, slice_size), bf),
        vmem((2, width, slice_size), bf),
        vmem((2, slice_size, width), bf),
        vmem((2, 256, slice_size), jnp.float32),
        vmem((2, 256, slice_size), jnp.float32),
        vmem((2, 256, slice_size), bf),
    ]
    blocks = (2, SIDE, SIDE, 16)
    for lead in ((nz, 16), blocks, blocks, (2, 2, 2, 16), (2, 2, 4, 16),
                 (2, 3, 16), (nz, 16), (nz, 16)):
        scratch += [vmem(lead + ((w if lead[0] == nz else 4 * w),), bf) for w in ws]
    scratch.append(dma((3,)))
    for shape in [(nk, nz - 1), (nk, 2, 3), (nk, 2, 2, 4), (nk, 2, 2),
                  (3,), (nk, 2, 2), (nk, 2, 2), (nk, 2, 2), (nk, 2, 3), (nk, nz - 1)]:
        scratch += [dma(shape), dma(shape)]
    any_spec = pl.BlockSpec(memory_space=pl.ANY)
    vmem_spec = pl.BlockSpec(memory_space=pltpu.VMEM)
    return pl.pallas_call(
        functools.partial(moe_kernel, ws, nz),
        out_shape=jax.ShapeDtypeStruct(outgoing.shape, bf),
        in_specs=[vmem_spec] + [any_spec] * 3,
        out_specs=vmem_spec,
        scratch_shapes=scratch,
        compiler_params=pltpu.CompilerParams(
            collective_id=0, has_side_effects=True, vmem_limit_bytes=60 * 1024 * 1024
        ),
    )(outgoing, w_gate, w_up, w_down)


def per_device(
    queries,
    cache_keys,
    cache_values,
    new_keys,
    new_values,
    lengths,
    residual,
    norm_gain,
    routes,
    gate_logits,
    w_gate,
    w_up,
    w_down,
):
    attended = attend(queries, cache_keys, cache_values, new_keys, new_values, lengths)
    mixed = residual.astype(jnp.float32) + attended.astype(jnp.float32)
    normed = (
        mixed * lax.rsqrt(jnp.mean(mixed * mixed, axis=-1, keepdims=True) + 1e-05) * norm_gain
    ).astype(jnp.bfloat16)
    nz = lax.axis_size("hid")
    width = normed.shape[1]
    ws = (256, 256, 256)
    expert_ids = jnp.arange(nz, dtype=jnp.int32)
    chosen = routes[:, :, None] == expert_ids[None, None, :]
    gates = jax.nn.softmax(gate_logits, axis=-1)
    combine = jnp.sum(jnp.where(chosen, gates[:, :, None], jnp.float32(0.0)), axis=1)
    selected = jnp.any(chosen, axis=1).astype(jnp.int32)
    ranking = jnp.cumsum(selected, axis=0) - selected
    slot_ids = jnp.arange(CAP, dtype=jnp.int32)
    placement = (selected.T[:, None, :] == 1) & (ranking.T[:, None, :] == slot_ids[None, :, None])
    outgoing = jnp.einsum(
        "ecr,rd->ecd", placement.astype(jnp.bfloat16), normed, preferred_element_type=jnp.float32
    ).astype(jnp.bfloat16)
    ends = [8 * sum(ws[: k + 1]) for k in range(len(ws))]
    outgoing = jnp.concatenate(
        [outgoing[:, :, end - 8 * w:end].reshape(nz, CAP * 8, w) for end, w in zip(ends, ws)],
        axis=-1,
    )
    returned = experts(outgoing, w_gate[0], w_up[0], w_down[0], ws)
    returned = jnp.concatenate(
        [
            returned[:, :, end // 8 - w:end // 8].reshape(nz, CAP, 8 * w)
            for end, w in zip(ends, ws)
        ],
        axis=-1,
    )
    mixing = placement.astype(jnp.float32) * combine.T[:, None, :]
    moe = jnp.einsum("ecr,ecd->rd", mixing, returned.astype(jnp.float32))
    return (mixed + moe).astype(jnp.bfloat16)


def solution(mesh):
    in_specs = (
        P(("grp", "exp", "hid"), None, None),
        P(("grp", "exp", "hid"), None, None, None),
        P(("grp", "exp", "hid"), None, None, None),
        P(("grp", "exp", "hid"), None, None),
        P(("grp", "exp", "hid"), None, None),
        P(("grp", "exp", "hid")),
        P(("grp", "exp", "hid"), None),
        P(),
        P(("grp", "exp", "hid"), None),
        P(("grp", "exp", "hid"), None),
        P("hid", None, ("grp", "exp")),
        P("hid", None, ("grp", "exp")),
        P("hid", ("grp", "exp"), None),
    )
    out_specs = P(("grp", "exp", "hid"), None)
    return jax.shard_map(
        per_device, mesh=mesh, in_specs=in_specs, out_specs=out_specs, check_vma=False
    )
```

```python
import functools
import math

import jax
import jax.numpy as jnp
from jax import lax
from jax.experimental import pallas as pl
from jax.experimental.pallas import tpu as pltpu
from jax.sharding import PartitionSpec as P

CAP = 2
CHOICES = 2
SIDE = 4
MESH = pl.DeviceIdType.MESH


def moe_kernel(ws, nz, *refs):
    bf = jnp.bfloat16
    f32 = jnp.float32
    nk = len(ws)
    chunks = range(nk)
    starts = [8 * sum(ws[:k]) for k in chunks]
    refs = list(refs)
    lanes = [pl.ds(start // 8, w) for start, w in zip(starts, ws)]

    def take(n):
        got = refs[:n]
        del refs[:n]
        return got

    (lens, routes, logits, queries, new_keys, new_values, residual, gain,
     keys_hbm, values_hbm, wg_hbm, wu_hbm, wd_hbm, out) = take(14)
    keys, values, mixed, normed, out_in = take(5)
    wg, wu, wd, acc_g, acc_u, hid = take(6)
    zin, xall, part, t1, t2, t3, zout, zret = [take(nk) for _ in range(8)]
    (kv_sem, w_sem, zs_s, zs_r, p1_s, p1_r, p2_s, p2_r, fw_s, fw_r,
     ws_s, ws_r, t1_s, t1_r, tf_s, tf_r, t2_s, t2_r, t3_s, t3_r, zo_s, zo_r) = refs

    g = lax.axis_index("grp")
    xy = lax.axis_index("exp")
    z = lax.axis_index("hid")
    x = xy // SIDE
    y = xy % SIDE

    def at_x(d):
        return (g, ((x + d) % SIDE) * SIDE + y, z)

    def at_y(d):
        return (g, x * SIDE + (y + d) % SIDE, z)

    def at_z(d):
        return (g, xy, (z + d) % nz)

    partner = (1 - g, xy, z)
    along = (at_x, at_y)
    across = (at_y, at_x)
    far_first = (2, 1, 3)
    z_far_first = sorted(range(1, nz), key=lambda d: -min(d, nz - d))

    sent = []

    def send(src, dst, ssem, rsem, dev):
        copy = pltpu.make_async_remote_copy(
            src_ref=src, dst_ref=dst, send_sem=ssem, recv_sem=rsem,
            device_id=dev, device_id_type=MESH,
        )
        copy.start()
        sent.append(copy)

    def landed(dst, ssem, rsem, dev):
        pltpu.make_async_remote_copy(
            src_ref=dst, dst_ref=dst, send_sem=ssem, recv_sem=rsem,
            device_id=dev, device_id_type=MESH,
        ).wait_recv()

    barrier = pltpu.get_barrier_semaphore()
    friends = [partner]
    friends += [at_x(d) for d in (1, 2, 3)] + [at_y(d) for d in (1, 2, 3)]
    friends += [at_z(d) for d in range(1, nz)]
    for dev in friends:
        pl.semaphore_signal(barrier, inc=1, device_id=dev, device_id_type=MESH)
    cache_copies = [
        pltpu.make_async_copy(keys_hbm, keys, kv_sem.at[0]),
        pltpu.make_async_copy(values_hbm, values, kv_sem.at[1]),
    ]
    for copy in cache_copies:
        copy.start()
    weights = ((wg_hbm, wg), (wu_hbm, wu), (wd_hbm, wd))
    own_weights = [
        pltpu.make_async_copy(src, dst.at[g], w_sem.at[n]) for n, (src, dst) in enumerate(weights)
    ]

    rows_dev, heads, size = queries.shape
    kv_heads = new_keys.shape[1]
    group = heads // kv_heads
    slots = keys.shape[1]

    def iota(shape, dim):
        return lax.broadcasted_iota(jnp.int32, shape, dim)

    def dot_t(a, b):
        return lax.dot_general(a, b, (((1,), (1,)), ((), ())), preferred_element_type=f32)

    def owns(shape):
        low = (iota(shape, 1) & (kv_heads - 1)) * group
        head = iota(shape, 0)
        return (head >= low) & (head < low + group)

    for n in range(heads):
        mixed[n * rows_dev:(n + 1) * rows_dev, :] = residual[:, n * size:(n + 1) * size].astype(f32)

    for copy in cache_copies:
        copy.wait()

    for i in range(rows_dev):
        scale = 1.0 / math.sqrt(size)
        wide = (heads, slots)
        valid = owns(wide) & (iota(wide, 1) < lens[i] * kv_heads)
        cached = jnp.where(valid, dot_t(queries[i], keys[i]) * scale, f32(-1e30))
        own = owns((heads, kv_heads))
        fresh = jnp.where(own, dot_t(queries[i], new_keys[i]) * scale, f32(0.0))
        fresh = jnp.sum(fresh, axis=1, keepdims=True)
        highest = jnp.maximum(jnp.max(cached, axis=1, keepdims=True), fresh)
        cached_exp = jnp.exp(cached - highest)
        fresh_exp = jnp.exp(fresh - highest)
        share = 1.0 / (jnp.sum(cached_exp, axis=1, keepdims=True) + fresh_exp)
        cached_w = (cached_exp * share).astype(bf)
        fresh_w = jnp.where(own, fresh_exp * share, f32(0.0)).astype(bf)
        attended = jnp.dot(cached_w, values[i], preferred_element_type=f32)
        attended = attended + jnp.dot(fresh_w, new_values[i], preferred_element_type=f32)
        request = pl.ds(i, heads, stride=rows_dev)
        mix = mixed[request, :] + attended.astype(bf).astype(f32)
        mixed[request, :] = mix
        square = jnp.sum(jnp.sum(mix * mix, axis=1, keepdims=True), axis=0, keepdims=True)
        norm = lax.rsqrt(square * (1.0 / (heads * size)) + 1e-05)
        normed[i] = (mix * norm * gain[...]).astype(bf)

    seat = []
    for i in range(rows_dev):
        for c in range(CHOICES):
            rank = jnp.int32(0)
            for before in range(i):
                for other in range(CHOICES):
                    rank = rank + jnp.where(routes[other, before] == routes[c, i], 1, 0)
            seat.append(routes[c, i] * CAP + rank)

    per = ws[0] // size
    pieces = 8 * per
    shape = (nz * 16, rows_dev * heads)
    seat_of = iota(shape, 0) >> 3
    part_of = iota(shape, 0) & 7
    piece = jnp.zeros(shape, jnp.int32)
    taken = jnp.zeros(shape, jnp.int32)
    for i in range(rows_dev):
        begin = iota(shape, 1) >= i * heads
        piece = jnp.where(begin, iota(shape, 1) - i * heads, piece)
        hit = jnp.zeros(shape, jnp.int32)
        for c in range(CHOICES):
            hit = jnp.where(seat_of == seat[i * CHOICES + c], 1, hit)
        taken = jnp.where(begin, hit, taken)
    piece = jnp.where(taken == 1, piece, -1)
    flat = normed[...].reshape(rows_dev * heads, size)
    for k in chunks:
        for j in range(per):
            pick = jnp.where(piece == k * pieces + part_of * per + j, f32(1.0), f32(0.0))
            block = jnp.dot(pick.astype(bf), flat, preferred_element_type=f32).astype(bf)
            start = (k * per + j) * size
            out_in[:, :, start:start + size] = block.reshape(nz, 16, size)

    shape = (pieces * rows_dev, nz * 16)
    seat_of = iota(shape, 1) >> 3
    part_of = iota(shape, 1) & 7
    piece = iota(shape, 0) // rows_dev
    request_of = iota(shape, 0) & (rows_dev - 1)
    level = [jnp.zeros(shape, f32) for _ in range(CHOICES)]
    place = [jnp.zeros(shape, jnp.int32) for _ in range(CHOICES)]
    for i in range(rows_dev):
        for c in range(CHOICES):
            level[c] = jnp.where(request_of == i, logits[c, i], level[c])
            place[c] = jnp.where(request_of == i, seat[i * CHOICES + c], place[c])
    top = jnp.maximum(level[0], level[1])
    level = [jnp.exp(v - top) for v in level]
    mixing = jnp.zeros(shape, f32)
    for c in range(CHOICES):
        mixing = mixing + jnp.where(seat_of == place[c], level[c] / (level[0] + level[1]), f32(0.0))
    weighted = []
    for j in range(per):
        term = jnp.where(piece == part_of * per + j, mixing, f32(0.0))
        split = []
        for _ in range(3):
            split.append(term.astype(bf))
            term = term - split[-1].astype(f32)
        weighted.append(jnp.concatenate(split, axis=0))

    pl.semaphore_wait(barrier, len(friends))

    for k in chunks:
        for d in z_far_first:
            to = (z + d) % nz
            send(out_in.at[to, :, lanes[k]], zin[k].at[z], zs_s.at[k, d - 1], zs_r.at[k, d - 1], at_z(d))
    for k in chunks:
        zin[k][z] = out_in[z, :, lanes[k]]
    for copy in own_weights:
        copy.start()
    for n, (src, dst) in enumerate(weights):
        send(src, dst.at[g], ws_s.at[n], ws_r.at[n], partner)

    def ready(n):
        dst = weights[n][1]
        own_weights[n].wait()
        landed(dst.at[1 - g], ws_s.at[n], ws_r.at[n], partner)

    units = nz * 16
    row = lax.broadcasted_iota(jnp.int32, (units, units), 0)
    col = lax.broadcasted_iota(jnp.int32, (units, units), 1)
    spread = (col == (row % 16) * 8 + row // 16).astype(bf)
    gather = (row == (col % 16) * 8 + col // 16).astype(bf)

    def mine_half(k, h, d, side):
        if h == 0:
            return xall[k].at[0, pl.ds(2 * side, 2), (y + d) % SIDE]
        return xall[k].at[1, (x + d) % SIDE, pl.ds(2 * side, 2)]

    def came(k, h, j, d):
        if h == 0:
            return xall[k].at[0, (x + SIDE - j) % SIDE, (y + d) % SIDE]
        return xall[k].at[1, (x + d) % SIDE, (y + SIDE - j) % SIDE]

    def pass_on(k, h, j):
        ref = came(k, h, j, 0)
        for n, d in ((0, 1), (1, 3)):
            send(ref, ref, p2_s.at[k, h, n, j], p2_r.at[k, h, n, j], across[h](d))

    def a0(k):
        w = ws[k]
        for d in z_far_first[::-1]:
            src = (z + nz - d) % nz
            landed(zin[k].at[src], zs_s.at[k, d - 1], zs_r.at[k, d - 1], at_z(nz - d))
        block = zin[k][...].reshape(units, w)
        block = jnp.dot(spread, block, preferred_element_type=f32).astype(bf)
        for n in range(8):
            h, q = n // 4, n % 4
            xall[k][h, x, y, :, q * w:(q + 1) * w] = block[n * 16:(n + 1) * 16]
        for h in range(2):
            for d in far_first:
                ref = xall[k].at[h, x, y]
                send(ref, ref, p1_s.at[k, h, d - 1], p1_r.at[k, h, d - 1], along[h](d))
        for h in range(2):
            pass_on(k, h, 0)

    def a1(k):
        for h in range(2):
            for d in (1, 3, 2):
                ref = came(k, h, d, 0)
                landed(ref, p1_s.at[k, h, d - 1], p1_r.at[k, h, d - 1], along[h](SIDE - d))
                pass_on(k, h, d)

    def a2(k):
        for h in range(2):
            for n, d in ((0, 3), (1, 1)):
                for j in (0, 1, 3, 2):
                    ref = came(k, h, j, d)
                    landed(ref, p2_s.at[k, h, n, j], p2_r.at[k, h, n, j], across[h](d))
                half = mine_half(k, h, d, n)
                send(half, half, fw_s.at[k, h, n], fw_r.at[k, h, n], across[h](SIDE - d))

    def a3(k):
        for h in range(2):
            for n, d in ((0, 3), (1, 1)):
                half = mine_half(k, h, 2, n)
                landed(half, fw_s.at[k, h, n], fw_r.at[k, h, n], across[h](d))

    def m(k):
        wide = 4 * ws[k]
        if k == 0:
            ready(0)
            ready(1)

        @pl.loop(0, 2)
        def _(i):
            gate, up = None, None
            for h in range(2):
                lhs = xall[k][h].reshape(256, wide)
                rows = slice(starts[k] + h * wide, starts[k] + (h + 1) * wide)
                a = jnp.dot(lhs, wg[i, rows, :], preferred_element_type=f32)
                b = jnp.dot(lhs, wu[i, rows, :], preferred_element_type=f32)
                gate = a if gate is None else gate + a
                up = b if up is None else up + b
            if k > 0:
                gate = gate + acc_g[i]
                up = up + acc_u[i]
            if k < nk - 1:
                acc_g[i] = gate
                acc_u[i] = up
            else:
                hid[i] = (gate * jax.nn.sigmoid(gate) * up).astype(bf)

    def down(k, h):
        wide = 4 * ws[k]
        cols = slice(starts[k] + h * wide, starts[k] + (h + 1) * wide)
        value = jnp.dot(hid[0], wd[0, :, cols], preferred_element_type=f32)
        value = value + jnp.dot(hid[1], wd[1, :, cols], preferred_element_type=f32)
        part[k][h] = value.astype(bf).reshape(SIDE, SIDE, 16, wide)

    def total(*terms):
        value = terms[0][...].astype(f32)
        for term in terms[1:]:
            value = value + term[...].astype(f32)
        return value.astype(bf)

    def block_of(buf, k, h, d):
        if h == 0:
            return buf[k].at[0, :, (y + d) % SIDE]
        return buf[k].at[1, (x + d) % SIDE]

    def half_of(buf, k, h, d, side):
        if h == 0:
            return buf[k].at[0, pl.ds(2 * side, 2), (y + d) % SIDE]
        return buf[k].at[1, (x + d) % SIDE, pl.ds(2 * side, 2)]

    def s1(k):
        if k == 0:
            ready(2)
        for h in range(2):
            down(k, h)
            for n, d in ((0, 1), (1, 3)):
                send(half_of(part, k, h, 2, n), t1[k].at[h, n], t1_s.at[k, h, n], t1_r.at[k, h, n], across[h](d))
            for n, d in ((0, 1), (1, 3)):
                send(half_of(part, k, h, d, 1 - n), t2[k].at[h, n, pl.ds(2 * (1 - n), 2)], tf_s.at[k, h, n], tf_r.at[k, h, n], across[h](d))

    def s2(k):
        for h in range(2):
            for n, d in ((0, 1), (1, 3)):
                landed(t1[k].at[h, n], t1_s.at[k, h, n], t1_r.at[k, h, n], across[h](SIDE - d))
                half = half_of(part, k, h, d, n)
                half[...] = total(half, t1[k].at[h, n])
                send(half, t2[k].at[h, n, pl.ds(2 * n, 2)], t2_s.at[k, h, n], t2_r.at[k, h, n], across[h](d))

    def s3(k):
        for h in range(2):
            for n, d in ((0, 1), (1, 3)):
                free = t2[k].at[h, n, pl.ds(2 * (1 - n), 2)]
                landed(free, tf_s.at[k, h, n], tf_r.at[k, h, n], across[h](SIDE - d))
                half = t2[k].at[h, n, pl.ds(2 * n, 2)]
                landed(half, t2_s.at[k, h, n], t2_r.at[k, h, n], across[h](SIDE - d))
            block = block_of(part, k, h, 0)
            block[...] = total(block, t2[k].at[h, 0], t2[k].at[h, 1])
            for d in far_first:
                if h == 0:
                    src = part[k].at[0, (x + d) % SIDE, y]
                else:
                    src = part[k].at[1, x, (y + d) % SIDE]
                send(src, t3[k].at[h, d - 1], t3_s.at[k, h, d - 1], t3_r.at[k, h, d - 1], along[h](d))

    def s4(k):
        w = ws[k]
        parts = []
        for h in range(2):
            for d in far_first[::-1]:
                landed(t3[k].at[h, d - 1], t3_s.at[k, h, d - 1], t3_r.at[k, h, d - 1], along[h](SIDE - d))
            value = total(part[k].at[h, x, y], *[t3[k].at[h, n] for n in range(3)])
            parts += [value[:, q * w:(q + 1) * w] for q in range(4)]
        block = jnp.concatenate(parts, axis=0)
        block = jnp.dot(gather, block, preferred_element_type=f32).astype(bf)
        zout[k][...] = block.reshape(nz, 16, w)
        for d in z_far_first:
            to = (z + d) % nz
            send(zout[k].at[to], zret[k].at[z], zo_s.at[k, d - 1], zo_r.at[k, d - 1], at_z(d))
        zret[k][z] = zout[k][z]

    def s5(k):
        for d in z_far_first[::-1]:
            src = (z + nz - d) % nz
            landed(zret[k].at[src], zo_s.at[k, d - 1], zo_r.at[k, d - 1], at_z(nz - d))
        block = zret[k][...].reshape(units, ws[k])
        moe = None
        for j in range(per):
            piece_sum = jnp.dot(
                weighted[j], block[:, j * size:(j + 1) * size], preferred_element_type=f32
            )
            moe = piece_sum if moe is None else moe + piece_sum
        count = rows_dev * pieces
        moe = moe[:count] + moe[count:2 * count] + moe[2 * count:]
        moe = moe + mixed[k * count:(k + 1) * count, :]
        for n in range(pieces):
            start = (k * pieces + n) * size
            out[:, start:start + size] = moe[n * rows_dev:(n + 1) * rows_dev].astype(bf)

    for stage in (a0, a1, a2):
        for k in chunks:
            stage(k)
    for k in chunks:
        a3(k)
        m(k)
    for stage in (s1, s2, s3, s4, s5):
        for k in chunks:
            stage(k)
    for copy in sent:
        copy.wait_send()


def layer(lens, routes, logits, queries, new_keys, new_values, residual, gain, keys, values,
          w_gate, w_up, w_down, ws, nz):
    nk = len(ws)
    width, slice_size = w_gate.shape
    bf = jnp.bfloat16
    dma = pltpu.SemaphoreType.DMA
    vmem = pltpu.VMEM
    scratch = [
        vmem(keys.shape, bf),
        vmem(values.shape, bf),
        vmem((queries.shape[0] * queries.shape[1], queries.shape[2]), jnp.float32),
        vmem(queries.shape, bf),
        vmem((nz, 16, sum(ws)), bf),
        vmem((2, width, slice_size), bf),
        vmem((2, width, slice_size), bf),
        vmem((2, slice_size, width), bf),
        vmem((2, 256, slice_size), jnp.float32),
        vmem((2, 256, slice_size), jnp.float32),
        vmem((2, 256, slice_size), bf),
    ]
    blocks = (2, SIDE, SIDE, 16)
    for lead in ((nz, 16), blocks, blocks, (2, 2, 2, 16), (2, 2, 4, 16),
                 (2, 3, 16), (nz, 16), (nz, 16)):
        scratch += [vmem(lead + ((w if lead[0] == nz else 4 * w),), bf) for w in ws]
    scratch += [dma((2,)), dma((3,))]
    for shape in [(nk, nz - 1), (nk, 2, 3), (nk, 2, 2, 4), (nk, 2, 2),
                  (3,), (nk, 2, 2), (nk, 2, 2), (nk, 2, 2), (nk, 2, 3), (nk, nz - 1)]:
        scratch += [dma(shape), dma(shape)]
    any_spec = pl.BlockSpec(memory_space=pl.ANY)
    vmem_spec = pl.BlockSpec(memory_space=pltpu.VMEM)
    return pl.pallas_call(
        functools.partial(moe_kernel, ws, nz),
        out_shape=jax.ShapeDtypeStruct(residual.shape, bf),
        in_specs=[pl.BlockSpec(memory_space=pltpu.SMEM)] * 3 + [vmem_spec] * 5 + [any_spec] * 5,
        out_specs=vmem_spec,
        scratch_shapes=scratch,
        compiler_params=pltpu.CompilerParams(
            collective_id=0, has_side_effects=True, vmem_limit_bytes=60 * 1024 * 1024
        ),
    )(lens, routes, logits, queries, new_keys, new_values, residual, gain, keys, values,
      w_gate, w_up, w_down)


def per_device(
    queries,
    cache_keys,
    cache_values,
    new_keys,
    new_values,
    lengths,
    residual,
    norm_gain,
    routes,
    gate_logits,
    w_gate,
    w_up,
    w_down,
):
    nz = lax.axis_size("hid")
    count, heads, size = queries.shape
    kv_heads = new_keys.shape[1]
    ws = (256, 256, 256)
    flat_cache = (count, cache_keys.shape[1] * kv_heads, size)
    return layer(
        lengths, routes.T, gate_logits.T, queries, new_keys, new_values, residual,
        norm_gain.reshape(heads, size),
        cache_keys.reshape(flat_cache), cache_values.reshape(flat_cache),
        w_gate[0], w_up[0], w_down[0], ws, nz,
    )


def solution(mesh):
    in_specs = (
        P(("grp", "exp", "hid"), None, None),
        P(("grp", "exp", "hid"), None, None, None),
        P(("grp", "exp", "hid"), None, None, None),
        P(("grp", "exp", "hid"), None, None),
        P(("grp", "exp", "hid"), None, None),
        P(("grp", "exp", "hid")),
        P(("grp", "exp", "hid"), None),
        P(),
        P(("grp", "exp", "hid"), None),
        P(("grp", "exp", "hid"), None),
        P("hid", None, ("grp", "exp")),
        P("hid", None, ("grp", "exp")),
        P("hid", ("grp", "exp"), None),
    )
    out_specs = P(("grp", "exp", "hid"), None)
    return jax.shard_map(
        per_device, mesh=mesh, in_specs=in_specs, out_specs=out_specs, check_vma=False
    )
```
